32 devices in a mesh: tm: 8 (over y, x, core), space: 4 (over z).
Axes of the slice: x: 2, y: 2, z: 4, core: 2. Of those that a mesh axis runs over, the one named last changes fastest.
Arguments:
- q_spatial: bfloat16 [8, 512, 1152], P('tm', 'space'), may hold values from -6 to 6
- k_spatial: bfloat16 [8, 512, 1152], P('tm', 'space'), may hold values from -6 to 6
- v_spatial: bfloat16 [8, 512, 1152], P('tm', 'space'), may hold values from -6 to 6
- grad_spatial: bfloat16 [8, 512, 1152], P('tm', 'space'), may hold values from -192 to 192
- q_temporal: bfloat16 [8, 512, 1152], P('tm', 'space'), may hold values from -6 to 6
- k_temporal: bfloat16 [8, 512, 1152], P('tm', 'space'), may hold values from -6 to 6
- v_temporal: bfloat16 [8, 512, 1152], P('tm', 'space'), may hold values from -6 to 6
- grad_temporal: bfloat16 [8, 512, 1152], P('tm', 'space'), may hold values from -24 to 24
Outputs:
- dq_spatial: bfloat16 [8, 512, 1152], P('tm', 'space')
- dk_spatial: bfloat16 [8, 512, 1152], P('tm', 'space')
- dv_spatial: bfloat16 [8, 512, 1152], P('tm', 'space')
- dq_temporal: bfloat16 [8, 512, 1152], P('tm', 'space')
- dk_temporal: bfloat16 [8, 512, 1152], P('tm', 'space')
- dv_temporal: bfloat16 [8, 512, 1152], P('tm', 'space')
The draws below stay inside these ranges and needn't reach their ends.
All inputs are finite; a program needn't handle non-finite values.
Results may differ from the reference program's by a relative error of at most 0.012.
The reference program's roundings to bfloat16 on the way count: a program that leaves them out, or rounds other values in their place, can miss the bound.
Values may be sent and summed in bfloat16 or wider, within the bound.
No kernel may reach another device: no remote copies, remote signals or barrier semaphores. Data moves between devices by JAX's collectives and lax.ppermute only.
A program may use at most 64 MiB of HBM per device.

```python
import math
import jax
import jax.numpy as jnp
from jax import lax

D = 1152
HEADS = 16
HEAD_DIM = 72
FRAMES = 8
FTOK = 512


def draw_q_spatial(key, part):
    key = jax.random.fold_in(key, 3)
    values = jnp.clip(jax.random.normal(key, (FRAMES, FTOK, D), jnp.float32), -6.0, 6.0)
    return values.astype(jnp.bfloat16)


def draw_k_spatial(key, part):
    key = jax.random.fold_in(key, 5)
    values = jnp.clip(jax.random.normal(key, (FRAMES, FTOK, D), jnp.float32), -6.0, 6.0)
    return values.astype(jnp.bfloat16)


def draw_q_temporal(key, part):
    key = jax.random.fold_in(key, 7)
    values = jnp.clip(jax.random.normal(key, (FRAMES, FTOK, D), jnp.float32), -6.0, 6.0)
    return values.astype(jnp.bfloat16)


def draw_k_temporal(key, part):
    key = jax.random.fold_in(key, 9)
    values = jnp.clip(jax.random.normal(key, (FRAMES, FTOK, D), jnp.float32), -6.0, 6.0)
    return values.astype(jnp.bfloat16)


def level_of(stream_key, dims, pieces, least, high):
    gain, own = 1.0, jax.random.fold_in(stream_key, 6)
    for dim, blocks in pieces:
        heights = jnp.exp(jax.random.uniform(jax.random.fold_in(own, dim), (blocks,), jnp.float32, least / len(pieces), high / len(pieces)))
        gain = gain * jnp.repeat(heights, dims[dim] // blocks).reshape([-1 if axis == dim else 1 for axis in range(len(dims))])
    return gain


def centred(rng, dims, scale, reach, cuts=(), held_as=jnp.bfloat16):
    values = jax.random.normal(rng, dims, jnp.float32) * scale
    if len(cuts) > 0:
        values = level_of(rng, dims, cuts, -0.22, 0.18) * values
    return jnp.clip(values, min=-reach, max=reach).astype(held_as)


def setup_inputs(seed: int = 0) -> dict:
    key_list = jax.random.split(jax.random.key(seed), 9)
    q_spatial = draw_q_spatial(jax.random.fold_in(key_list[8], 71), 0)
    k_spatial = draw_k_spatial(jax.random.fold_in(key_list[8], 71), 0)
    v_spatial = centred(key_list[2], (FRAMES, FTOK, D), 1.0, 6.0, ((0, 8), (1, 4)))
    grad_spatial = centred(key_list[3], (FRAMES, FTOK, D), 32.0, 192.0, ((0, 8), (1, 4)))
    q_temporal = draw_q_temporal(jax.random.fold_in(key_list[8], 71), 0)
    k_temporal = draw_k_temporal(jax.random.fold_in(key_list[8], 71), 0)
    v_temporal = centred(key_list[6], (FRAMES, FTOK, D), 1.0, 6.0, ((0, 8), (1, 4)))
    grad_temporal = centred(key_list[7], (FRAMES, FTOK, D), 4.0, 24.0, ((0, 8), (1, 4)))
    return dict(q_spatial=q_spatial, k_spatial=k_spatial, v_spatial=v_spatial, grad_spatial=grad_spatial, q_temporal=q_temporal, k_temporal=k_temporal, v_temporal=v_temporal, grad_temporal=grad_temporal)


def head_pass(queries, keys_in, values_in, grads_in):
    width = queries.shape[1]
    score_scale = 1.0 / math.sqrt(width)
    scores = jnp.dot(queries, keys_in.T, preferred_element_type=jnp.float32) * score_scale
    peak = lax.optimization_barrier(jnp.max(scores, axis=-1, keepdims=True))
    raised = jnp.exp(scores - peak)
    probs = raised / lax.optimization_barrier(jnp.sum(raised, axis=-1, keepdims=True))
    weights = probs.astype(jnp.bfloat16)
    outputs = jnp.dot(weights, values_in, preferred_element_type=jnp.float32)
    delta_rows = lax.optimization_barrier(jnp.sum(grads_in.astype(jnp.float32) * outputs, axis=-1, keepdims=True))
    dv_rows = jnp.dot(weights.T, grads_in, preferred_element_type=jnp.float32).astype(jnp.bfloat16)
    dprobs = jnp.dot(grads_in, values_in.T, preferred_element_type=jnp.float32)
    dscores = (probs * (dprobs - delta_rows)).astype(jnp.bfloat16)
    dq_rows = (jnp.dot(dscores, keys_in, preferred_element_type=jnp.float32) * score_scale).astype(jnp.bfloat16)
    dk_rows = (jnp.dot(dscores.T, queries, preferred_element_type=jnp.float32) * score_scale).astype(jnp.bfloat16)
    return (dq_rows, dk_rows, dv_rows)

def frame_heads(parts):

    def one_head(head_parts):
        return head_pass(head_parts[0], head_parts[1], head_parts[2], head_parts[3])
    return lax.map(one_head, parts)

def spatial_reference(queries, keys_in, values_in, grads_in):

    def split_heads(array):
        return array.reshape(FRAMES, FTOK, HEADS, HEAD_DIM).transpose(0, 2, 1, 3)

    def merge_heads(array):
        return array.transpose(0, 2, 1, 3).reshape(FRAMES, FTOK, HEADS * HEAD_DIM)
    results = lax.map(frame_heads, (split_heads(queries), split_heads(keys_in), split_heads(values_in), split_heads(grads_in)))
    return (merge_heads(results[0]), merge_heads(results[1]), merge_heads(results[2]))

def temporal_reference(queries, keys_in, values_in, grads_in):

    def split_heads(array):
        return array.reshape(FRAMES, FTOK, HEADS, HEAD_DIM).transpose(1, 2, 0, 3)

    def merge_heads(array):
        return array.transpose(2, 0, 1, 3).reshape(FRAMES, FTOK, HEADS * HEAD_DIM)
    mapped = jax.vmap(jax.vmap(head_pass))
    results = mapped(split_heads(queries), split_heads(keys_in), split_heads(values_in), split_heads(grads_in))
    return (merge_heads(results[0]), merge_heads(results[1]), merge_heads(results[2]))

def reference(q_spatial, k_spatial, v_spatial, grad_spatial, q_temporal, k_temporal, v_temporal, grad_temporal):
    dq_spatial, dk_spatial, dv_spatial = spatial_reference(q_spatial, k_spatial, v_spatial, grad_spatial)
    dq_temporal, dk_temporal, dv_temporal = temporal_reference(q_temporal, k_temporal, v_temporal, grad_temporal)
    return (dq_spatial, dk_spatial, dv_spatial, dq_temporal, dk_temporal, dv_temporal)
```

```python
import functools
import math

import jax
import jax.numpy as jnp
from jax import lax
from jax.experimental import pallas as pl
from jax.experimental.pallas import tpu as pltpu
from jax.sharding import PartitionSpec as P

HEAD_DIM = 72
SCALE = 1.0 / math.sqrt(HEAD_DIM)
EXP2_SCALE = SCALE * math.log2(math.e)
LANES = 128
CHUNKS = 1

NT = (((1,), (1,)), ((), ()))
TN = (((0,), (0,)), ((), ()))
VMEM_LIMIT = 48 * 1024 * 1024


def call(kernel, out_shape, *, flops=0, moved=0, exps=0, scratch=()):
    return pl.pallas_call(
        kernel,
        out_shape=out_shape,
        scratch_shapes=list(scratch),
        compiler_params=pltpu.CompilerParams(vmem_limit_bytes=VMEM_LIMIT),
        cost_estimate=pl.CostEstimate(flops=flops, bytes_accessed=moved, transcendentals=exps),
    )


def bf16(*shape):
    return jax.ShapeDtypeStruct(shape, jnp.bfloat16)


def swap(array, axis, distance):
    size = lax.axis_size(axis)
    return lax.ppermute(array, axis, [(i, i ^ distance) for i in range(size)])


def spatial_pack_kernel(group, chunks, *refs):
    sources, outs, scratch = refs[:4], refs[4:-1], refs[-1]
    share = scratch.shape[2]
    for a in range(4):
        turned = sources[a][...].T
        for d in range(group):
            scratch[a, d] = turned[d * share : (d + 1) * share]
    me = lax.axis_index("space")
    rows = share // chunks
    for k in range(group):
        to = me ^ k
        for a in range(4):
            block = scratch[a, to]
            for c in range(chunks):
                outs[k * chunks + c][a * rows : (a + 1) * rows] = block[c * rows : (c + 1) * rows]


def spatial_core_kernel(heads, *refs):
    group = (len(refs)) // 2
    messages, outs = refs[:group], refs[group:]
    whole = jnp.concatenate([m[...] for m in messages], axis=1)
    length = whole.shape[1]
    block = min(512, length)
    per = LANES
    for h in range(heads):
        qs, ks, vs, gs = (
            whole[(a * heads + h) * HEAD_DIM : (a * heads + h + 1) * HEAD_DIM] for a in range(4)
        )
        k_rows, v_rows = ks.T, vs.T
        dk = jnp.zeros((HEAD_DIM, length), jnp.float32)
        dv = jnp.zeros((HEAD_DIM, length), jnp.float32)
        dqs = []
        for b in range(length // block):
            q = qs[:, b * block : (b + 1) * block]
            g = gs[:, b * block : (b + 1) * block]
            s = jnp.dot(k_rows, q, preferred_element_type=jnp.float32)
            e = jnp.exp2((s - jnp.max(s, axis=0, keepdims=True)) * EXP2_SCALE)
            p = e * (1.0 / jnp.sum(e, axis=0, keepdims=True))
            w = p.astype(jnp.bfloat16)
            dp = jnp.dot(v_rows, g, preferred_element_type=jnp.float32)
            delta = jnp.sum(w.astype(jnp.float32) * dp, axis=0, keepdims=True)
            ds = (p * (dp - delta)).astype(jnp.bfloat16)
            dqs.append(jnp.dot(ks, ds, preferred_element_type=jnp.float32))
            dk += lax.dot_general(q, ds, NT, preferred_element_type=jnp.float32)
            dv += lax.dot_general(g, w, NT, preferred_element_type=jnp.float32)
        dq = jnp.concatenate(dqs, axis=1)
        for i, result in enumerate((dq * SCALE, dk * SCALE, dv)):
            low = result.astype(jnp.bfloat16)
            row = (i * heads + h) * HEAD_DIM
            for k in range(group):
                outs[k][row : row + HEAD_DIM] = low[:, k * per : (k + 1) * per]


def spatial_unpack_kernel(group, chunks, *refs):
    messages, outs, scratch = refs[: group * chunks], refs[group * chunks : -1], refs[-1]
    share = scratch.shape[2]
    rows = share // chunks
    me = lax.axis_index("space")
    for k in range(group):
        of = me ^ k
        parts = [messages[k * chunks + c][...] for c in range(chunks)]
        for i in range(3):
            scratch[i, of] = jnp.concatenate([p[i * rows : (i + 1) * rows] for p in parts], axis=0)
    for i in range(3):
        outs[i][...] = scratch[i].reshape(group * share, LANES).T


def spatial(q, k, v, g):
    tokens, width = q.shape
    group = lax.axis_size("space")
    share = width // group
    heads_here = share // HEAD_DIM
    chunks = math.gcd(CHUNKS, heads_here)
    heads = heads_here // chunks
    nbytes = 4 * tokens * width * 2
    packed = call(
        functools.partial(spatial_pack_kernel, group, chunks),
        [bf16(4 * heads * HEAD_DIM, tokens)] * (group * chunks),
        moved=2 * nbytes,
        scratch=[pltpu.VMEM((4, group, share, tokens), jnp.bfloat16)],
    )(q, k, v, g)
    length = group * tokens
    back = [[None] * chunks for _ in range(group)]
    for c in range(chunks):
        arrived = [
            packed[d * chunks + c] if d == 0 else swap(packed[d * chunks + c], "space", d)
            for d in range(group)
        ]
        results = call(
            functools.partial(spatial_core_kernel, heads),
            [bf16(3 * heads * HEAD_DIM, tokens)] * group,
            flops=2 * 5 * heads * length * length * HEAD_DIM,
            exps=heads * length * length,
            moved=7 * heads * HEAD_DIM * length * 2,
        )(*arrived)
        for d in range(group):
            back[d][c] = results[d] if d == 0 else swap(results[d], "space", d)
    return call(
        functools.partial(spatial_unpack_kernel, group, chunks),
        [bf16(tokens, width)] * 3,
        moved=2 * nbytes * 3 // 4,
        scratch=[pltpu.VMEM((3, group, share, tokens), jnp.bfloat16)],
    )(*[m for row in back for m in row])


def temporal_pack_kernel(group, *refs):
    sources, outs = refs[:4], refs[4:]
    me = lax.axis_index("tm")
    rows = outs[0].shape[1]
    for k in range(group):
        start = pl.multiple_of((me ^ k) * rows, rows)
        for a in range(4):
            outs[k][a] = sources[a][pl.ds(start, rows)]


def temporal_core_kernel(*refs):
    group = len(refs) // 2
    messages, outs = refs[:group], refs[group:]
    tok = messages[0].shape[1]
    width = messages[0].shape[2]
    total = group * tok
    arrays = [jnp.concatenate([m[a] for m in messages], axis=0) for a in range(4)]
    row = lax.broadcasted_iota(jnp.int32, (total, total), 0)
    col = lax.broadcasted_iota(jnp.int32, (total, total), 1)
    same = lax.rem(row, tok) == lax.rem(col, tok)
    lane = lax.broadcasted_iota(jnp.int32, (total, LANES), 1)
    tiles = width // LANES
    sums = [[[] for _ in range(tiles)] for _ in range(3)]

    def flush(t):
        for i in range(3):
            left = [x for x, _ in sums[i][t]]
            right = jnp.concatenate([y for _, y in sums[i][t]], axis=0)
            if i == 0:
                lhs = jnp.concatenate(left, axis=0)
                value = lax.dot_general(lhs, right, TN, preferred_element_type=jnp.float32)
            else:
                lhs = jnp.concatenate(left, axis=1)
                value = jnp.dot(lhs, right, preferred_element_type=jnp.float32)
            if i < 2:
                value = value * SCALE
            low = value.astype(jnp.bfloat16)
            for k in range(group):
                outs[k][i, :, t * LANES : (t + 1) * LANES] = low[k * tok : (k + 1) * tok]

    for h in range(width // HEAD_DIM):
        first, last = h * HEAD_DIM, (h + 1) * HEAD_DIM - 1
        span = range(first // LANES, last // LANES + 1)

        def part(a, t, masked=True):
            block = arrays[a][:, t * LANES : (t + 1) * LANES]
            if not masked:
                return block
            lo, hi = first - t * LANES, last - t * LANES
            keep = (lane >= lo) & (lane <= hi)
            return jnp.where(keep, block, jnp.zeros_like(block))

        qm = [part(0, t) for t in span]
        km = [part(1, t) for t in span]
        gm = [part(3, t) for t in span]
        s = lax.dot_general(
            jnp.concatenate(km, axis=1), jnp.concatenate(qm, axis=1), NT, preferred_element_type=jnp.float32
        )
        dp = lax.dot_general(
            jnp.concatenate([part(2, t, False) for t in span], axis=1),
            jnp.concatenate(gm, axis=1),
            NT,
            preferred_element_type=jnp.float32,
        )
        s = jnp.where(same, s, -1e30)
        e = jnp.exp2((s - jnp.max(s, axis=0, keepdims=True)) * EXP2_SCALE)
        p = e * (1.0 / jnp.sum(e, axis=0, keepdims=True))
        w = p.astype(jnp.bfloat16)
        delta = jnp.sum(w.astype(jnp.float32) * dp, axis=0, keepdims=True)
        ds = (p * (dp - delta)).astype(jnp.bfloat16)
        for j, t in enumerate(span):
            sums[0][t].append((ds, km[j]))
            sums[1][t].append((ds, qm[j]))
            sums[2][t].append((w, gm[j]))
            if (t + 1) * LANES <= last + 1:
                flush(t)


def temporal_unpack_kernel(*refs):
    group = len(refs) - 3
    messages, outs = refs[:group], refs[group:]
    me = lax.axis_index("tm")
    rows = messages[0].shape[1]
    for k in range(group):
        start = pl.multiple_of((me ^ k) * rows, rows)
        for i in range(3):
            outs[i][pl.ds(start, rows)] = messages[k][i]


def temporal(q, k, v, g):
    tokens, width = q.shape
    group = lax.axis_size("tm")
    rows = tokens // group
    aligned = rows % 16 == 0
    nbytes = 4 * tokens * width * 2
    partner = lax.axis_index("tm") ^ jnp.arange(group)
    if aligned:
        packed = call(
            functools.partial(temporal_pack_kernel, group),
            [bf16(4, rows, width)] * group,
            moved=2 * nbytes,
        )(q, k, v, g)
    else:
        stacked = jnp.stack([x.reshape(group, rows, width) for x in (q, k, v, g)], axis=1)
        packed = [
            lax.dynamic_index_in_dim(stacked, partner[d], 0, keepdims=False) for d in range(group)
        ]
    arrived = [packed[d] if d == 0 else swap(packed[d], "tm", d) for d in range(group)]
    results = call(
        temporal_core_kernel,
        [bf16(3, rows, width)] * group,
        flops=2 * 5 * 2 * tokens * tokens * width,
        exps=tokens * tokens * width // HEAD_DIM,
        moved=nbytes * 7 // 4,
    )(*arrived)
    back = [results[d] if d == 0 else swap(results[d], "tm", d) for d in range(group)]
    if aligned:
        return call(
            temporal_unpack_kernel, [bf16(tokens, width)] * 3, moved=2 * nbytes * 3 // 4
        )(*back)
    stacked = jnp.take(jnp.stack(back), partner, axis=0)
    return [stacked[:, i].reshape(tokens, width) for i in range(3)]


def shards(*arrays):
    local = [array[0] for array in arrays]
    results = list(spatial(*local[:4])) + list(temporal(*local[4:]))
    return tuple(result[None] for result in results)


def solution(mesh):
    placed = P("tm", "space", None)
    return jax.shard_map(
        shards,
        mesh=mesh,
        in_specs=(placed,) * 8,
        out_specs=(placed,) * 6,
        check_vma=False,
    )
```

```python
import functools
import math

import jax
import jax.numpy as jnp
from jax import lax
from jax.experimental import pallas as pl
from jax.experimental.pallas import tpu as pltpu
from jax.sharding import PartitionSpec as P

HEAD_DIM = 72
SCALE = 1.0 / math.sqrt(HEAD_DIM)
EXP2_SCALE = SCALE * math.log2(math.e)
LANES = 128
CHUNKS = 2
HOLD = False
HEAD_GROUP = 8
IN_ORDER = "desc"
OUT_ORDER = "desc"
COST = {"core_spatial0": 20, "core_spatial1": 10, "core_temporal": 3, "unpack_spatial": 3, "pack_temporal": 5}
AFTER = 1
LAST = ""
VM = {"pack_spatial": 63}

NT = (((1,), (1,)), ((), ()))
TN = (((0,), (0,)), ((), ()))
VMEM_LIMIT = 48 * 1024 * 1024


def call(name, kernel, out_shape, *, us=1.0, scratch=(), **specs):
    return pl.pallas_call(
        kernel,
        out_shape=out_shape,
        scratch_shapes=list(scratch),
        **specs,
        name=name,
        compiler_params=pltpu.CompilerParams(vmem_limit_bytes=VM.get(name, 48) * 1024 * 1024),
        cost_estimate=pl.CostEstimate(
            flops=int(COST.get(name, us) * 1e9), bytes_accessed=1024, transcendentals=0
        ),
    )


def bf16(*shape):
    return jax.ShapeDtypeStruct(shape, jnp.bfloat16)


def swap(array, axis, distance):
    size = lax.axis_size(axis)
    return lax.ppermute(array, axis, [(i, i ^ distance) for i in range(size)])


def spatial_pack_kernel(group, chunks, *refs):
    sources, outs, token = refs[:4], refs[4:-4], refs[-4]
    scratch, staged, sems = refs[-3:]
    share = scratch.shape[2]
    copies = [
        pltpu.make_async_copy(sources[a].at[0], staged.at[a], sems.at[a]) for a in range(4)
    ]
    for copy in copies:
        copy.start()
    token[...] = jnp.zeros_like(token)
    for a in range(4):
        copies[a].wait()
        turned = staged[a].T
        for d in range(group):
            scratch[a, d] = turned[d * share : (d + 1) * share]
    me = lax.axis_index("space")
    rows = share // chunks
    for k in range(group):
        to = me ^ k
        for a in range(4):
            block = scratch[a, to]
            for c in range(chunks):
                outs[k * chunks + c][a * rows : (a + 1) * rows] = block[c * rows : (c + 1) * rows]


def spatial_core_kernel(heads, *refs):
    group = (len(refs)) // 2
    messages, outs = refs[:group], refs[group:]
    whole = jnp.concatenate([m[...] for m in messages], axis=1)
    length = whole.shape[1]
    block = min(512, length)
    per = length // group
    every = range(heads)

    def mm(x, y):
        return jnp.dot(x, y, preferred_element_type=jnp.float32)

    def nt(x, y):
        return lax.dot_general(x, y, NT, preferred_element_type=jnp.float32)

    qs, ks, vs, gs = (
        [whole[(a * heads + h) * HEAD_DIM : (a * heads + h + 1) * HEAD_DIM] for h in every]
        for a in range(4)
    )
    k_rows = [x.T for x in ks]
    v_rows = [x.T for x in vs]
    dk = [jnp.zeros((HEAD_DIM, length), jnp.float32)] * heads
    dv = [jnp.zeros((HEAD_DIM, length), jnp.float32)] * heads
    dqs = [[] for h in every]
    for b in range(length // block):
        q = [x[:, b * block : (b + 1) * block] for x in qs]
        g = [x[:, b * block : (b + 1) * block] for x in gs]
        s = [mm(x, y) for x, y in zip(k_rows, q)]
        dp = [mm(x, y) for x, y in zip(v_rows, g)]
        for h in every:
            e = jnp.exp2((s[h] - jnp.max(s[h], axis=0, keepdims=True)) * EXP2_SCALE)
            p = e * (1.0 / jnp.sum(e, axis=0, keepdims=True))
            w = p.astype(jnp.bfloat16)
            delta = jnp.sum(w.astype(jnp.float32) * dp[h], axis=0, keepdims=True)
            ds = (p * (dp[h] - delta)).astype(jnp.bfloat16)
            dqs[h].append(mm(ks[h], ds))
            dk[h] += nt(q[h], ds)
            dv[h] += nt(g[h], w)
    for h in every:
        dq = jnp.concatenate(dqs[h], axis=1)
        for i, result in enumerate((dq * SCALE, dk[h] * SCALE, dv[h])):
            low = result.astype(jnp.bfloat16)
            row = (i * heads + h) * HEAD_DIM
            for k in range(group):
                outs[k][row : row + HEAD_DIM] = low[:, k * per : (k + 1) * per]


def spatial_unpack_kernel(places, chunks, *refs):
    group = len(places)
    messages, outs, scratch = refs[: group * chunks], refs[group * chunks : -1], refs[-1]
    share = scratch.shape[2]
    rows = share // chunks
    me = lax.axis_index("space")
    for k, d in enumerate(places):
        of = me ^ d
        parts = [messages[c * group + k][...] for c in range(chunks)]
        for i in range(3):
            scratch[i, of] = jnp.concatenate([p[i * rows : (i + 1) * rows] for p in parts], axis=0)
    for i in range(3):
        outs[i][...] = scratch[i].reshape(group * share, LANES).T


def spatial_send(q, k, v, g):
    _, tokens, width = q.shape
    group = lax.axis_size("space")
    share = width // group
    heads_here = share // HEAD_DIM
    chunks = math.gcd(CHUNKS, heads_here)
    heads = heads_here // chunks
    *packed, token = call(
        "pack_spatial",
        functools.partial(spatial_pack_kernel, group, chunks),
        [bf16(4 * heads * HEAD_DIM, tokens)] * (group * chunks) + [bf16(16, LANES)],
        in_specs=[pl.BlockSpec(memory_space=pltpu.HBM)] * 4,
        scratch=[
            pltpu.VMEM((4, group, share, tokens), jnp.bfloat16),
            pltpu.VMEM((4, tokens, width), jnp.bfloat16),
            pltpu.SemaphoreType.DMA((4,)),
        ],
    )(q, k, v, g)
    arrived = []
    for c in range(chunks):
        far = [swap(packed[d * chunks + c], "space", d) for d in range(group - 1, 0, -1)]
        arrived.append([packed[c]] + far[::-1])
    return arrived, token


def order(kind, group):
    far = list(range(1, group))
    if kind == "desc":
        far = far[::-1]
    elif kind != "asc" and len(kind) == group - 1:
        far = [int(c) for c in kind]
    return [0] + far


def spatial_core(arrived, first):
    if not arrived:
        return []
    group = len(arrived[0])
    places = order(IN_ORDER, group)
    rows, tokens = arrived[0][0].shape
    heads = rows // (4 * HEAD_DIM)
    length = group * tokens
    results = []
    for c, messages in enumerate(arrived):
        results.append(
            call(
            f"core_spatial{first + c}",
            functools.partial(spatial_core_kernel, heads),
            [bf16(3 * heads * HEAD_DIM, tokens)] * group,
            us=1.2 * heads * (length / 512) ** 2,
        )(*[messages[d] for d in places])
        )
    return [[chunk[places.index(d)] for d in range(group)] for chunk in results]


def spatial_return(results, width):
    chunks, group = len(results), len(results[0])
    tokens = results[0][0].shape[1]
    places = order(OUT_ORDER, group)
    back = []
    for mine in results:
        far = [swap(mine[d], "space", d) for d in range(group - 1, 0, -1)]
        back.append([mine[0]] + far[::-1])
    return call(
        "unpack_spatial",
        functools.partial(spatial_unpack_kernel, places, chunks),
        [bf16(tokens, width)] * 3,
        scratch=[pltpu.VMEM((3, group, width // group, tokens), jnp.bfloat16)],
    )(*[back[c][d] for c in range(chunks) for d in places]), back


def temporal_pack_kernel(q, k, v, g, token, out):
    group, _, rows, _ = out.shape
    for t in range(group):
        for a, source in enumerate((q, k, v, g)):
            out[t, a] = source[0, t * rows : (t + 1) * rows]


def temporal_core_kernel(messages, token, out):
    group, _, tok, width = messages.shape
    total = group * tok
    arrays = [
        jnp.concatenate([messages[t, a] for t in range(group)], axis=0) for a in range(4)
    ]
    row = lax.broadcasted_iota(jnp.int32, (total, total), 0)
    col = lax.broadcasted_iota(jnp.int32, (total, total), 1)
    same = lax.rem(row, tok) == lax.rem(col, tok)
    lane = lax.broadcasted_iota(jnp.int32, (total, LANES), 1)
    tiles = width // LANES
    sums = [[[] for _ in range(tiles)] for _ in range(3)]

    def flush(t):
        for i in range(3):
            left = [x for x, _ in sums[i][t]]
            right = jnp.concatenate([y for _, y in sums[i][t]], axis=0)
            if i == 0:
                lhs = jnp.concatenate(left, axis=0)
                value = lax.dot_general(lhs, right, TN, preferred_element_type=jnp.float32)
            else:
                lhs = jnp.concatenate(left, axis=1)
                value = jnp.dot(lhs, right, preferred_element_type=jnp.float32)
            if i < 2:
                value = value * SCALE
            low = value.astype(jnp.bfloat16)
            for k in range(group):
                out[k, i, :, t * LANES : (t + 1) * LANES] = low[k * tok : (k + 1) * tok]

    def part(a, h, t, masked=True):
        block = arrays[a][:, t * LANES : (t + 1) * LANES]
        if not masked:
            return block
        low = h * HEAD_DIM - t * LANES
        keep = (lane >= low) & (lane < low + HEAD_DIM)
        return jnp.where(keep, block, jnp.zeros_like(block))

    def wide(parts):
        return jnp.concatenate(parts, axis=1)

    heads = width // HEAD_DIM
    for start in range(0, heads, HEAD_GROUP):
        batch = range(start, min(start + HEAD_GROUP, heads))
        spans = [range(h * HEAD_DIM // LANES, ((h + 1) * HEAD_DIM - 1) // LANES + 1) for h in batch]
        qm = [[part(0, h, t) for t in span] for h, span in zip(batch, spans)]
        km = [[part(1, h, t) for t in span] for h, span in zip(batch, spans)]
        gm = [[part(3, h, t) for t in span] for h, span in zip(batch, spans)]
        vs = [[part(2, h, t, False) for t in span] for h, span in zip(batch, spans)]
        s = [
            lax.dot_general(wide(x), wide(y), NT, preferred_element_type=jnp.float32)
            for x, y in zip(km, qm)
        ]
        dp = [
            lax.dot_general(wide(x), wide(y), NT, preferred_element_type=jnp.float32)
            for x, y in zip(vs, gm)
        ]
        s = [jnp.where(same, x, -1e30) for x in s]
        e = [jnp.exp2((x - jnp.max(x, axis=0, keepdims=True)) * EXP2_SCALE) for x in s]
        p = [x * (1.0 / jnp.sum(x, axis=0, keepdims=True)) for x in e]
        w = [x.astype(jnp.bfloat16) for x in p]
        delta = [
            jnp.sum(x.astype(jnp.float32) * y, axis=0, keepdims=True) for x, y in zip(w, dp)
        ]
        ds = [(x * (y - z)).astype(jnp.bfloat16) for x, y, z in zip(p, dp, delta)]
        for n, h in enumerate(batch):
            for j, t in enumerate(spans[n]):
                sums[0][t].append((ds[n], km[n][j]))
                sums[1][t].append((ds[n], qm[n][j]))
                sums[2][t].append((w[n], gm[n][j]))
                if (t + 1) * LANES <= (h + 1) * HEAD_DIM:
                    flush(t)


def temporal_unpack_kernel(*refs):
    messages, outs, sems = refs[0], refs[-4:-1], refs[-1]
    group, _, rows, _ = messages.shape
    copies = [
        pltpu.make_async_copy(
            messages.at[t, i], outs[i].at[0, t * rows : (t + 1) * rows], sems.at[t, i]
        )
        for i in range(3)
        for t in range(group)
    ]
    for copy in copies:
        copy.start()
    for copy in copies:
        copy.wait()


def temporal_send(q, k, v, g, token):
    _, tokens, width = q.shape
    group = lax.axis_size("tm")
    rows = tokens // group
    if rows % 16 == 0:
        packed = call(
            "pack_temporal",
            temporal_pack_kernel,
            bf16(group, 4, rows, width),
            in_specs=[pl.BlockSpec(memory_space=pltpu.VMEM)] * 4
            + [pl.BlockSpec(memory_space=pl.ANY)],
        )(q, k, v, g, token)
    else:
        packed = jnp.stack([x.reshape(group, rows, width) for x in (q, k, v, g)], axis=1)
    return lax.all_to_all(packed, "tm", 0, 0, tiled=True)


def temporal_core(arrived, token):
    group, _, rows, width = arrived.shape
    return call(
        "core_temporal",
        temporal_core_kernel,
        bf16(group, 3, rows, width),
        us=3.4,
        in_specs=[pl.BlockSpec(memory_space=pltpu.VMEM), pl.BlockSpec(memory_space=pl.ANY)],
    )(arrived, token)


def temporal_return(results, last):
    group, _, rows, width = results.shape
    arrived = lax.all_to_all(results, "tm", 0, 0, tiled=True)
    if rows % 16 == 0:
        return call(
            "unpack_temporal",
            temporal_unpack_kernel,
            [bf16(1, group * rows, width)] * 3,
            in_specs=[pl.BlockSpec(memory_space=pl.ANY)] * (1 + len(last)),
            out_specs=[pl.BlockSpec(memory_space=pltpu.HBM)] * 3,
            scratch=[pltpu.SemaphoreType.DMA((group, 3))],
        )(arrived, *last)
    return [arrived[:, i].reshape(1, group * rows, width) for i in range(3)]


def shards(*arrays):
    width = arrays[0].shape[2]
    spatial_in, token = spatial_send(*arrays[:4])
    temporal_in = temporal_send(*arrays[4:], token)
    cut = len(spatial_in) if AFTER is None else min(AFTER, len(spatial_in))
    spatial_out = spatial_core(spatial_in[:cut], 0)
    temporal_out = temporal_core(temporal_in, spatial_out[-1][0] if cut else token)
    if cut < len(spatial_in):
        if HOLD:
            spatial_in[cut][0], _ = lax.optimization_barrier((spatial_in[cut][0], temporal_out))
        spatial_out += spatial_core(spatial_in[cut:], cut)
    spatial_grads, zback = spatial_return(spatial_out, width)
    last = {"uz": spatial_grads[:1], "z1": zback[0][1:2], "z12": zback[0][1:3], "z13": zback[0][1:4:2], "": []}[LAST]
    temporal_grads = temporal_return(temporal_out, last)
    return tuple(x[None] for x in spatial_grads) + tuple(temporal_grads)


def solution(mesh):
    placed = P("tm", "space", None)
    return jax.shard_map(
        shards,
        mesh=mesh,
        in_specs=(placed,) * 8,
        out_specs=(placed,) * 6,
        check_vma=False,
    )
```

```python
import functools
import math

import jax
import jax.numpy as jnp
from jax import lax
from jax.experimental import pallas as pl
from jax.experimental.pallas import tpu as pltpu
from jax.sharding import PartitionSpec as P

HEAD_DIM = 72
SCALE = 1.0 / math.sqrt(HEAD_DIM)
EXP2_SCALE = SCALE * math.log2(math.e)
LANES = 128
CHUNKS = 2
REST_AFTER = True
HOLD = True
HEAD_GROUP = 8
IN_ORDER = "213"
OUT_ORDER = "231"
SEND_ORDER = "desc"
COST = {"core_spatial0": 40, "core_spatial1": 15, "core_temporal": 3, "unpack": 3}
AFTER = 1
VM = {"pack_spatial": 62}

NT = (((1,), (1,)), ((), ()))
TN = (((0,), (0,)), ((), ()))
VMEM_LIMIT = 48 * 1024 * 1024


def call(name, kernel, out_shape, *, us=1.0, scratch=(), **specs):
    return pl.pallas_call(
        kernel,
        out_shape=out_shape,
        scratch_shapes=list(scratch),
        **specs,
        name=name,
        compiler_params=pltpu.CompilerParams(vmem_limit_bytes=VM.get(name, 48) * 1024 * 1024),
        cost_estimate=pl.CostEstimate(
            flops=int(COST.get(name, us) * 1e9), bytes_accessed=1024, transcendentals=0
        ),
    )


def bf16(*shape):
    return jax.ShapeDtypeStruct(shape, jnp.bfloat16)


def swap(array, axis, distance):
    size = lax.axis_size(axis)
    return lax.ppermute(array, axis, [(i, i ^ distance) for i in range(size)])


def cut_messages(turned, outs, group, chunks, wanted):
    me = lax.axis_index("space")
    rows = turned.shape[2] // chunks
    for n, c in enumerate(wanted):
        for d in range(group):
            for a in range(4):
                block = turned[a, me ^ d]
                outs[n * group + d][a * rows : (a + 1) * rows] = block[c * rows : (c + 1) * rows]


def spatial_pack_kernel(group, chunks, *refs):
    sources, outs, turned = refs[:4], refs[4 : 4 + group], refs[-3]
    staged, sems = refs[-2:]
    share = turned.shape[2]
    copies = [
        pltpu.make_async_copy(sources[a].at[0], staged.at[a], sems.at[a]) for a in range(4)
    ]
    for copy in copies:
        copy.start()
    for a in range(4):
        copies[a].wait()
        block = staged[a].T
        for d in range(group):
            turned[a, d] = block[d * share : (d + 1) * share]
    cut_messages(turned, outs, group, chunks, [0])


def spatial_pack_rest_kernel(group, chunks, turned, token, *outs):
    cut_messages(turned, outs, group, chunks, range(1, chunks))


def temporal_pack_kernel(q, k, v, g, token, out):
    group, _, rows, _ = out.shape
    for t in range(group):
        for a, source in enumerate((q, k, v, g)):
            out[t, a] = source[0, t * rows : (t + 1) * rows]


def spatial_core_kernel(heads, *refs):
    group = (len(refs)) // 2
    messages, outs = refs[:group], refs[group:]
    whole = jnp.concatenate([m[...] for m in messages], axis=1)
    length = whole.shape[1]
    block = min(512, length)
    per = length // group
    every = range(heads)

    def mm(x, y):
        return jnp.dot(x, y, preferred_element_type=jnp.float32)

    def nt(x, y):
        return lax.dot_general(x, y, NT, preferred_element_type=jnp.float32)

    qs, ks, vs, gs = (
        [whole[(a * heads + h) * HEAD_DIM : (a * heads + h + 1) * HEAD_DIM] for h in every]
        for a in range(4)
    )
    k_rows = [x.T for x in ks]
    v_rows = [x.T for x in vs]
    dk = [jnp.zeros((HEAD_DIM, length), jnp.float32)] * heads
    dv = [jnp.zeros((HEAD_DIM, length), jnp.float32)] * heads
    dqs = [[] for h in every]
    for b in range(length // block):
        q = [x[:, b * block : (b + 1) * block] for x in qs]
        g = [x[:, b * block : (b + 1) * block] for x in gs]
        s = [mm(x, y) for x, y in zip(k_rows, q)]
        dp = [mm(x, y) for x, y in zip(v_rows, g)]
        for h in every:
            e = jnp.exp2((s[h] - jnp.max(s[h], axis=0, keepdims=True)) * EXP2_SCALE)
            p = e * (1.0 / jnp.sum(e, axis=0, keepdims=True))
            w = p.astype(jnp.bfloat16)
            delta = jnp.sum(w.astype(jnp.float32) * dp[h], axis=0, keepdims=True)
            ds = (p * (dp[h] - delta)).astype(jnp.bfloat16)
            dqs[h].append(mm(ks[h], ds))
            dk[h] += nt(q[h], ds)
            dv[h] += nt(g[h], w)
    for h in every:
        dq = jnp.concatenate(dqs[h], axis=1)
        for i, result in enumerate((dq * SCALE, dk[h] * SCALE, dv[h])):
            low = result.astype(jnp.bfloat16)
            row = (i * heads + h) * HEAD_DIM
            for k in range(group):
                outs[k][row : row + HEAD_DIM] = low[:, k * per : (k + 1) * per]


def unpack_kernel(places, chunks, *refs):
    group = len(places)
    messages, others = refs[: group * chunks], refs[group * chunks : -4]
    scratch, turned, sems, other_sems = refs[-4:]
    outs, slices = others[-3:], []
    if len(others) > 3:
        arrived, outs = others[0], others[1:4]
        parts, _, rows, _ = arrived.shape
        slices = [
            pltpu.make_async_copy(
                arrived.at[t, i], others[4 + i].at[0, t * rows : (t + 1) * rows], other_sems.at[t, i]
            )
            for i in range(3)
            for t in range(parts)
        ]
    for copy in slices:
        copy.start()
    share, tokens = scratch.shape[2:]
    rows = share // chunks
    me = lax.axis_index("space")
    copies = []
    for i in range(3):
        for k, d in enumerate(places):
            parts = [
                messages[c * group + k][i * rows : (i + 1) * rows] for c in range(chunks)
            ]
            scratch[i, me ^ d] = jnp.concatenate(parts, axis=0)
        turned[i] = scratch[i].reshape(group * share, tokens).T
        copies.append(pltpu.make_async_copy(turned.at[i], outs[i].at[0], sems.at[i]))
        copies[i].start()
    for copy in copies + slices:
        copy.wait()


def send(arrays):
    _, tokens, width = arrays[0].shape
    group, parts = lax.axis_size("space"), lax.axis_size("tm")
    share = width // group
    heads_here = share // HEAD_DIM
    chunks = math.gcd(CHUNKS, heads_here)
    rows = tokens // parts
    hbm, vmem = pl.BlockSpec(memory_space=pltpu.HBM), pl.BlockSpec(memory_space=pltpu.VMEM)
    message = bf16(4 * share // chunks, tokens)
    *messages, turned = call(
        "pack_spatial",
        functools.partial(spatial_pack_kernel, group, chunks),
        [message] * group + [bf16(4, group, share, tokens)],
        in_specs=[hbm] * 4,
        scratch=[
            pltpu.VMEM((4, tokens, width), jnp.bfloat16),
            pltpu.SemaphoreType.DMA((4,)),
        ],
    )(*arrays[:4])
    if rows % 16 == 0:
        slices = call(
            "pack_temporal",
            temporal_pack_kernel,
            bf16(parts, 4, rows, width),
            in_specs=[vmem] * 4 + [pl.BlockSpec(memory_space=pl.ANY)],
        )(*arrays[4:], messages[0])
    else:
        slices = jnp.stack([x.reshape(parts, rows, width) for x in arrays[4:]], axis=1)
    if chunks > 1:
        messages += call(
            "pack_rest",
            functools.partial(spatial_pack_rest_kernel, group, chunks),
            [message] * (group * (chunks - 1)),
            in_specs=[vmem, pl.BlockSpec(memory_space=pl.ANY)],
        )(turned, slices if REST_AFTER else messages[0])
    spatial = []
    for c in range(chunks):
        mine = messages[c * group : (c + 1) * group]
        far = {d: swap(mine[d], "space", d) for d in order(SEND_ORDER, group)[1:]}
        spatial.append([mine[0]] + [far[d] for d in range(1, group)])
    return spatial, lax.all_to_all(slices, "tm", 0, 0, tiled=True)


def order(kind, group):
    far = list(range(1, group))
    if kind == "desc":
        far = far[::-1]
    elif kind != "asc" and len(kind) == group - 1:
        far = [int(c) for c in kind]
    return [0] + far


def spatial_core(arrived, first):
    if not arrived:
        return []
    group = len(arrived[0])
    places = order(IN_ORDER, group)
    rows, tokens = arrived[0][0].shape
    heads = rows // (4 * HEAD_DIM)
    length = group * tokens
    results = []
    for c, messages in enumerate(arrived):
        results.append(
            call(
            f"core_spatial{first + c}",
            functools.partial(spatial_core_kernel, heads),
            [bf16(3 * heads * HEAD_DIM, tokens)] * group,
            us=1.2 * heads * (length / 512) ** 2,
        )(*[messages[d] for d in places])
        )
    return [[chunk[places.index(d)] for d in range(group)] for chunk in results]


def give_back(spatial, temporal, width):
    chunks, group = len(spatial), len(spatial[0])
    tokens = spatial[0][0].shape[1]
    parts, _, rows, _ = temporal.shape
    aligned = rows % 16 == 0
    places = order(OUT_ORDER, group)
    messages = [
        mine[d] if d == 0 else swap(mine[d], "space", d) for mine in spatial for d in places
    ]
    arrived = lax.all_to_all(temporal, "tm", 0, 0, tiled=True)
    hbm, vmem = pl.BlockSpec(memory_space=pltpu.HBM), pl.BlockSpec(memory_space=pltpu.VMEM)
    outs = call(
        "unpack",
        functools.partial(unpack_kernel, places, chunks),
        [bf16(1, tokens, width)] * (6 if aligned else 3),
        in_specs=[vmem] * len(messages) + [pl.BlockSpec(memory_space=pl.ANY)] * aligned,
        out_specs=[hbm] * (6 if aligned else 3),
        scratch=[
            pltpu.VMEM((3, group, width // group, tokens), jnp.bfloat16),
            pltpu.VMEM((3, tokens, width), jnp.bfloat16),
            pltpu.SemaphoreType.DMA((3,)),
            pltpu.SemaphoreType.DMA((parts, 3)),
        ],
    )(*messages, *[arrived] * aligned)
    if aligned:
        return outs
    return list(outs) + [arrived[:, i].reshape(1, tokens, width) for i in range(3)]


def temporal_core_kernel(messages, token, out):
    group, _, tok, width = messages.shape
    total = group * tok
    arrays = [
        jnp.concatenate([messages[t, a] for t in range(group)], axis=0) for a in range(4)
    ]
    row = lax.broadcasted_iota(jnp.int32, (total, total), 0)
    col = lax.broadcasted_iota(jnp.int32, (total, total), 1)
    same = lax.rem(row, tok) == lax.rem(col, tok)
    lane = lax.broadcasted_iota(jnp.int32, (total, LANES), 1)
    tiles = width // LANES
    sums = [[[] for _ in range(tiles)] for _ in range(3)]

    def flush(t):
        for i in range(3):
            left = [x for x, _ in sums[i][t]]
            right = jnp.concatenate([y for _, y in sums[i][t]], axis=0)
            if i == 0:
                lhs = jnp.concatenate(left, axis=0)
                value = lax.dot_general(lhs, right, TN, preferred_element_type=jnp.float32)
            else:
                lhs = jnp.concatenate(left, axis=1)
                value = jnp.dot(lhs, right, preferred_element_type=jnp.float32)
            if i < 2:
                value = value * SCALE
            low = value.astype(jnp.bfloat16)
            for k in range(group):
                out[k, i, :, t * LANES : (t + 1) * LANES] = low[k * tok : (k + 1) * tok]

    def part(a, h, t, masked=True):
        block = arrays[a][:, t * LANES : (t + 1) * LANES]
        if not masked:
            return block
        low = h * HEAD_DIM - t * LANES
        keep = (lane >= low) & (lane < low + HEAD_DIM)
        return jnp.where(keep, block, jnp.zeros_like(block))

    def wide(parts):
        return jnp.concatenate(parts, axis=1)

    heads = width // HEAD_DIM
    for start in range(0, heads, HEAD_GROUP):
        batch = range(start, min(start + HEAD_GROUP, heads))
        spans = [range(h * HEAD_DIM // LANES, ((h + 1) * HEAD_DIM - 1) // LANES + 1) for h in batch]
        qm = [[part(0, h, t) for t in span] for h, span in zip(batch, spans)]
        km = [[part(1, h, t) for t in span] for h, span in zip(batch, spans)]
        gm = [[part(3, h, t) for t in span] for h, span in zip(batch, spans)]
        vs = [[part(2, h, t, False) for t in span] for h, span in zip(batch, spans)]
        s = [
            lax.dot_general(wide(x), wide(y), NT, preferred_element_type=jnp.float32)
            for x, y in zip(km, qm)
        ]
        dp = [
            lax.dot_general(wide(x), wide(y), NT, preferred_element_type=jnp.float32)
            for x, y in zip(vs, gm)
        ]
        s = [jnp.where(same, x, -1e30) for x in s]
        e = [jnp.exp2((x - jnp.max(x, axis=0, keepdims=True)) * EXP2_SCALE) for x in s]
        p = [x * (1.0 / jnp.sum(x, axis=0, keepdims=True)) for x in e]
        w = [x.astype(jnp.bfloat16) for x in p]
        delta = [
            jnp.sum(x.astype(jnp.float32) * y, axis=0, keepdims=True) for x, y in zip(w, dp)
        ]
        ds = [(x * (y - z)).astype(jnp.bfloat16) for x, y, z in zip(p, dp, delta)]
        for n, h in enumerate(batch):
            for j, t in enumerate(spans[n]):
                sums[0][t].append((ds[n], km[n][j]))
                sums[1][t].append((ds[n], qm[n][j]))
                sums[2][t].append((w[n], gm[n][j]))
                if (t + 1) * LANES <= (h + 1) * HEAD_DIM:
                    flush(t)


def temporal_core(arrived, token):
    group, _, rows, width = arrived.shape
    return call(
        "core_temporal",
        temporal_core_kernel,
        bf16(group, 3, rows, width),
        us=3.4,
        in_specs=[pl.BlockSpec(memory_space=pltpu.VMEM), pl.BlockSpec(memory_space=pl.ANY)],
    )(arrived, token)


def shards(*arrays):
    width = arrays[0].shape[2]
    spatial, temporal = send(arrays)
    cut = min(AFTER, len(spatial))
    done = spatial_core(spatial[:cut], 0)
    results = temporal_core(temporal, done[-1][0])
    if cut < len(spatial):
        if HOLD:
            spatial[cut][0], _ = lax.optimization_barrier((spatial[cut][0], results))
        done += spatial_core(spatial[cut:], cut)
    return tuple(give_back(done, results, width))


def solution(mesh):
    placed = P("tm", "space", None)
    return jax.shard_map(
        shards,
        mesh=mesh,
        in_specs=(placed,) * 8,
        out_specs=(placed,) * 6,
        check_vma=False,
    )
```

```python
import functools
import math

import jax
import jax.numpy as jnp
from jax import lax
from jax.experimental import pallas as pl
from jax.experimental.pallas import tpu as pltpu
from jax.sharding import PartitionSpec as P

HEAD_DIM = 72
SCALE = 1.0 / math.sqrt(HEAD_DIM)
EXP2_SCALE = SCALE * math.log2(math.e)
LANES = 128
SPLIT = (2, 2)
AHEAD = 1
GATE = (1,)
IN_ORDER = (3, 1, 2)
OUT_ORDER = (2, 1, 3)
HEAD_GROUP = 16
COST = {"core_spatial0": 40, "core_spatial1": 15, "core_temporal": 3, "unpack": 3}
VM = {"pack_spatial0": 62}

NT = (((1,), (1,)), ((), ()))
TN = (((0,), (0,)), ((), ()))
VMEM_LIMIT = 48 * 1024 * 1024


def call(name, kernel, out_shape, *, cost=1.0, scratch=(), **specs):
    return pl.pallas_call(
        kernel,
        out_shape=out_shape,
        scratch_shapes=list(scratch),
        **specs,
        name=name,
        compiler_params=pltpu.CompilerParams(vmem_limit_bytes=VM.get(name, 48) * 1024 * 1024),
        cost_estimate=pl.CostEstimate(
            flops=int(COST.get(name, cost) * 1e9), bytes_accessed=1024, transcendentals=0
        ),
    )


def bf16(*shape):
    return jax.ShapeDtypeStruct(shape, jnp.bfloat16)


def swap(array, axis, distance):
    size = lax.axis_size(axis)
    return lax.ppermute(array, axis, [(i, i ^ distance) for i in range(size)])


def spatial_pack_kernel(first, last, group, *refs):
    sources, outs = refs[:4], refs[-3 - group : -3]
    staged, turned, sems = refs[-3:]
    start = first // LANES * LANES
    share = turned.shape[2]
    copies = [
        pltpu.make_async_copy(
            sources[a].at[0, :, start : start + staged.shape[2]], staged.at[a], sems.at[a]
        )
        for a in range(4)
    ]
    for copy in copies:
        copy.start()
    for a in range(4):
        copies[a].wait()
        block = staged[a].T[first - start : last - start]
        for d in range(group):
            turned[a, d] = block[d * share : (d + 1) * share]
    me = lax.axis_index("space")
    for d in range(group):
        for a in range(4):
            outs[d][a * share : (a + 1) * share] = turned[a, me ^ d]


def temporal_pack_kernel(q, k, v, g, token, out):
    group, _, rows, _ = out.shape
    for t in range(group):
        for a, source in enumerate((q, k, v, g)):
            out[t, a] = source[0, t * rows : (t + 1) * rows]


def spatial_core_kernel(heads, *refs):
    group = (len(refs)) // 2
    messages, outs = refs[:group], refs[group:]
    whole = jnp.concatenate([m[...] for m in messages], axis=1)
    length = whole.shape[1]
    block = min(512, length)
    per = length // group
    every = range(heads)

    def mm(x, y):
        return jnp.dot(x, y, preferred_element_type=jnp.float32)

    def nt(x, y):
        return lax.dot_general(x, y, NT, preferred_element_type=jnp.float32)

    qs, ks, vs, gs = (
        [whole[(a * heads + h) * HEAD_DIM : (a * heads + h + 1) * HEAD_DIM] for h in every]
        for a in range(4)
    )
    k_rows = [x.T for x in ks]
    v_rows = [x.T for x in vs]
    dk = [jnp.zeros((HEAD_DIM, length), jnp.float32)] * heads
    dv = [jnp.zeros((HEAD_DIM, length), jnp.float32)] * heads
    dqs = [[] for h in every]
    for b in range(length // block):
        q = [x[:, b * block : (b + 1) * block] for x in qs]
        g = [x[:, b * block : (b + 1) * block] for x in gs]
        s = [mm(x, y) for x, y in zip(k_rows, q)]
        dp = [mm(x, y) for x, y in zip(v_rows, g)]
        for h in every:
            e = jnp.exp2((s[h] - jnp.max(s[h], axis=0, keepdims=True)) * EXP2_SCALE)
            p = e * (1.0 / jnp.sum(e, axis=0, keepdims=True))
            w = p.astype(jnp.bfloat16)
            delta = jnp.sum(w.astype(jnp.float32) * dp[h], axis=0, keepdims=True)
            ds = (p * (dp[h] - delta)).astype(jnp.bfloat16)
            dqs[h].append(mm(ks[h], ds))
            dk[h] += nt(q[h], ds)
            dv[h] += nt(g[h], w)
    for h in every:
        dq = jnp.concatenate(dqs[h], axis=1)
        for i, result in enumerate((dq * SCALE, dk[h] * SCALE, dv[h])):
            low = result.astype(jnp.bfloat16)
            row = (i * heads + h) * HEAD_DIM
            for k in range(group):
                outs[k][row : row + HEAD_DIM] = low[:, k * per : (k + 1) * per]


def temporal_unpack_kernel(arrived, *refs):
    outs, token, sems = refs[:3], refs[3], refs[4]
    parts, _, rows, _ = arrived.shape
    copies = [
        pltpu.make_async_copy(
            arrived.at[t, i], outs[i].at[0, t * rows : (t + 1) * rows], sems.at[t, i]
        )
        for i in range(3)
        for t in range(parts)
    ]
    for copy in copies:
        copy.start()
    token[...] = jnp.zeros_like(token)
    for copy in copies:
        copy.wait()


def spatial_unpack_kernel(first, last, group, count, *refs):
    messages, outs = refs[: group * count], refs[-5 - count : -2 - count]
    scratch, turned, sems = refs[-2 - count : -2], refs[-2], refs[-1]
    me = lax.axis_index("space")
    places = order(OUT_ORDER, group)
    copies = []
    for i in range(3):
        blocks = []
        for c in range(count):
            rows = scratch[c].shape[2]
            for k, d in enumerate(places):
                scratch[c][i, me ^ d] = messages[c * group + k][i * rows : (i + 1) * rows]
            blocks.append(scratch[c][i].reshape(group * rows, scratch[c].shape[3]))
        turned[i] = jnp.concatenate(blocks, axis=0)[first:last].T
        copies.append(
            pltpu.make_async_copy(turned.at[i], outs[i].at[0, :, first:last], sems.at[i])
        )
        copies[i].start()
    for copy in copies:
        copy.wait()


def send(arrays):
    _, tokens, width = arrays[0].shape
    group, parts = lax.axis_size("space"), lax.axis_size("tm")
    heads_here = width // HEAD_DIM // group
    split = SPLIT if sum(SPLIT) == heads_here else (heads_here,)
    chunks = len(split)
    rows = tokens // parts
    hbm, vmem = pl.BlockSpec(memory_space=pltpu.HBM), pl.BlockSpec(memory_space=pltpu.VMEM)
    later = pl.BlockSpec(memory_space=pl.ANY)

    def pack(c, *after):
        share = split[c] * HEAD_DIM
        first = group * HEAD_DIM * sum(split[:c])
        last = first + group * share
        span = -(-last // LANES) * LANES - first // LANES * LANES
        return call(
            f"pack_spatial{c}",
            functools.partial(spatial_pack_kernel, first, last, group),
            [bf16(4 * share, tokens)] * group,
            in_specs=[hbm] * 4 + [later] * len(after),
            scratch=[
                pltpu.VMEM((4, tokens, span), jnp.bfloat16),
                pltpu.VMEM((4, group, share, tokens), jnp.bfloat16),
                pltpu.SemaphoreType.DMA((4,)),
            ],
        )(*arrays[:4], *after)

    messages = pack(0)
    if rows % 16 == 0:
        slices = call(
            "pack_temporal",
            temporal_pack_kernel,
            bf16(parts, 4, rows, width),
            in_specs=[vmem] * 4 + [later],
        )(*arrays[4:], messages[0])
    else:
        slices = jnp.stack([x.reshape(parts, rows, width) for x in arrays[4:]], axis=1)
    for c in range(1, chunks):
        messages += pack(c, slices)
    spatial = []
    for c in range(chunks):
        mine = messages[c * group : (c + 1) * group]
        spatial.append([mine[0]] + [swap(mine[d], "space", d) for d in range(1, group)])
    return spatial, lax.all_to_all(slices, "tm", 0, 0, tiled=True)


def order(far, group):
    return [0, *(far if len(far) == group - 1 else range(1, group))]


def spatial_core(arrived, first):
    if not arrived:
        return []
    group = len(arrived[0])
    places = order(IN_ORDER, group)
    rows, tokens = arrived[0][0].shape
    heads = rows // (4 * HEAD_DIM)
    length = group * tokens
    results = []
    for c, messages in enumerate(arrived):
        results.append(
            call(
            f"core_spatial{first + c}",
            functools.partial(spatial_core_kernel, heads),
            [bf16(3 * heads * HEAD_DIM, tokens)] * group,
            cost=1.2 * heads * (length / 512) ** 2,
        )(*[messages[d] for d in places])
        )
    return [[chunk[places.index(d)] for d in range(group)] for chunk in results]


def give_back(spatial, temporal, width):
    chunks, group = len(spatial), len(spatial[0])
    tokens = spatial[0][0].shape[1]
    parts, _, rows, _ = temporal.shape
    places = order(OUT_ORDER, group)
    messages = [
        [mine[d] if d == 0 else swap(mine[d], "space", d) for d in places] for mine in spatial
    ]
    arrived = lax.all_to_all(temporal, "tm", 0, 0, tiled=True)
    hbm, vmem = pl.BlockSpec(memory_space=pltpu.HBM), pl.BlockSpec(memory_space=pltpu.VMEM)
    later = pl.BlockSpec(memory_space=pl.ANY)
    whole = [bf16(1, tokens, width)] * 3

    def unpack(name, first, last, mine, into, *after):
        n = len(mine) * group
        return call(
            name,
            functools.partial(spatial_unpack_kernel, first, last, group, len(mine)),
            whole,
            in_specs=[vmem] * n + [hbm] * len(into) + [later] * len(after),
            out_specs=[hbm] * 3,
            input_output_aliases={n + i: i for i in range(len(into))},
            scratch=[
                pltpu.VMEM((3, group, row[0].shape[0] // 3, tokens), jnp.bfloat16) for row in mine
            ]
            + [
                pltpu.VMEM((3, tokens, last - first), jnp.bfloat16),
                pltpu.SemaphoreType.DMA((3,)),
            ],
        )(*[m for row in mine for m in row], *into, *after)

    edge, begun = 0, []
    if chunks > 1:
        edge = (width - group * spatial[-1][0].shape[0] // 3) // LANES * LANES
        begun = unpack("unpack_early", 0, edge, messages[:-1], [])
    if rows % 16 == 0:
        *others, token = call(
            "unpack_temporal",
            temporal_unpack_kernel,
            whole + [bf16(16, LANES)],
            in_specs=[later],
            out_specs=[hbm] * 3 + [vmem],
            scratch=[pltpu.SemaphoreType.DMA((parts, 3))],
        )(arrived)
        after = [token]
    else:
        others = [arrived[:, i].reshape(1, tokens, width) for i in range(3)]
        after = []
    done = unpack("unpack", edge, width, messages, begun, *after)
    return list(done) + list(others)


def temporal_core_kernel(messages, *refs):
    out = refs[-1]
    group, _, tok, width = messages.shape
    total = group * tok
    arrays = [
        jnp.concatenate([messages[t, a] for t in range(group)], axis=0) for a in range(4)
    ]
    row = lax.broadcasted_iota(jnp.int32, (total, total), 0)
    col = lax.broadcasted_iota(jnp.int32, (total, total), 1)
    same = lax.rem(row, tok) == lax.rem(col, tok)
    lane = lax.broadcasted_iota(jnp.int32, (total, LANES), 1)
    tiles = width // LANES
    sums = [[[] for _ in range(tiles)] for _ in range(3)]

    def flush(t):
        for i in range(3):
            left = [x for x, _ in sums[i][t]]
            right = jnp.concatenate([y for _, y in sums[i][t]], axis=0)
            if i == 0:
                lhs = jnp.concatenate(left, axis=0)
                value = lax.dot_general(lhs, right, TN, preferred_element_type=jnp.float32)
            else:
                lhs = jnp.concatenate(left, axis=1)
                value = jnp.dot(lhs, right, preferred_element_type=jnp.float32)
            if i < 2:
                value = value * SCALE
            low = value.astype(jnp.bfloat16)
            for k in range(group):
                out[k, i, :, t * LANES : (t + 1) * LANES] = low[k * tok : (k + 1) * tok]

    def part(a, h, t, masked=True):
        block = arrays[a][:, t * LANES : (t + 1) * LANES]
        if not masked:
            return block
        low = h * HEAD_DIM - t * LANES
        keep = (lane >= low) & (lane < low + HEAD_DIM)
        return jnp.where(keep, block, jnp.zeros_like(block))

    def wide(parts):
        return jnp.concatenate(parts, axis=1)

    heads = width // HEAD_DIM
    for start in range(0, heads, HEAD_GROUP):
        batch = range(start, min(start + HEAD_GROUP, heads))
        spans = [range(h * HEAD_DIM // LANES, ((h + 1) * HEAD_DIM - 1) // LANES + 1) for h in batch]
        qm = [[part(0, h, t) for t in span] for h, span in zip(batch, spans)]
        km = [[part(1, h, t) for t in span] for h, span in zip(batch, spans)]
        gm = [[part(3, h, t) for t in span] for h, span in zip(batch, spans)]
        vs = [[part(2, h, t, False) for t in span] for h, span in zip(batch, spans)]
        s = [
            lax.dot_general(wide(x), wide(y), NT, preferred_element_type=jnp.float32)
            for x, y in zip(km, qm)
        ]
        dp = [
            lax.dot_general(wide(x), wide(y), NT, preferred_element_type=jnp.float32)
            for x, y in zip(vs, gm)
        ]
        s = [jnp.where(same, x, -1e30) for x in s]
        e = [jnp.exp2((x - jnp.max(x, axis=0, keepdims=True)) * EXP2_SCALE) for x in s]
        p = [x * (1.0 / jnp.sum(x, axis=0, keepdims=True)) for x in e]
        w = [x.astype(jnp.bfloat16) for x in p]
        delta = [
            jnp.sum(x.astype(jnp.float32) * y, axis=0, keepdims=True) for x, y in zip(w, dp)
        ]
        ds = [(x * (y - z)).astype(jnp.bfloat16) for x, y, z in zip(p, dp, delta)]
        for n, h in enumerate(batch):
            for j, t in enumerate(spans[n]):
                sums[0][t].append((ds[n], km[n][j]))
                sums[1][t].append((ds[n], qm[n][j]))
                sums[2][t].append((w[n], gm[n][j]))
                if (t + 1) * LANES <= (h + 1) * HEAD_DIM:
                    flush(t)


def temporal_core(arrived, after):
    group, _, rows, width = arrived.shape
    return call(
        "core_temporal",
        temporal_core_kernel,
        bf16(group, 3, rows, width),
        cost=3.4,
        in_specs=[pl.BlockSpec(memory_space=pltpu.VMEM)]
        + [pl.BlockSpec(memory_space=pl.ANY)] * len(after),
    )(arrived, *after)


def shards(*arrays):
    width = arrays[0].shape[2]
    spatial, temporal = send(arrays)
    cut = min(AHEAD, len(spatial))
    done = spatial_core(spatial[:cut], 0)
    after = [done[-1][0]]
    if cut < len(spatial):
        after += [spatial[cut][d] for d in GATE]
    results = temporal_core(temporal, after)
    if cut < len(spatial):
        spatial[cut][0], _ = lax.optimization_barrier((spatial[cut][0], results))
        done += spatial_core(spatial[cut:], cut)
    return tuple(give_back(done, results, width))


def solution(mesh):
    placed = P("tm", "space", None)
    return jax.shard_map(
        shards,
        mesh=mesh,
        in_specs=(placed,) * 8,
        out_specs=(placed,) * 6,
        check_vma=False,
    )
```

```python
import functools
import math

import jax
import jax.numpy as jnp
from jax import lax
from jax.experimental import pallas as pl
from jax.experimental.pallas import tpu as pltpu
from jax.sharding import PartitionSpec as P

HEAD_DIM = 72
SCALE = 1.0 / math.sqrt(HEAD_DIM)
EXP2_SCALE = SCALE * math.log2(math.e)
LANES = 128
SPLIT = (2, 2)
AHEAD = 1
GATE = (1,)
IN_ORDER = (3, 1, 2)
OUT_ORDER = (2, 1, 3)
HEAD_GROUP = 16
COST = {"core_spatial0": 40, "core_spatial1": 15, "core_temporal": 3, "unpack": 3}
VM = {"pack_spatial0": 62}

NT = (((1,), (1,)), ((), ()))
TN = (((0,), (0,)), ((), ()))
VMEM_LIMIT = 48 * 1024 * 1024


def call(name, kernel, out_shape, *, cost=1.0, scratch=(), **specs):
    return pl.pallas_call(
        kernel,
        out_shape=out_shape,
        scratch_shapes=list(scratch),
        **specs,
        name=name,
        compiler_params=pltpu.CompilerParams(vmem_limit_bytes=VM.get(name, 48) * 1024 * 1024),
        cost_estimate=pl.CostEstimate(
            flops=int(COST.get(name, cost) * 1e9), bytes_accessed=1024, transcendentals=0
        ),
    )


def bf16(*shape):
    return jax.ShapeDtypeStruct(shape, jnp.bfloat16)


def swap(array, axis, distance):
    size = lax.axis_size(axis)
    return lax.ppermute(array, axis, [(i, i ^ distance) for i in range(size)])


def spatial_pack_kernel(first, last, group, *refs):
    sources, outs = refs[:4], refs[-3 - group : -3]
    staged, turned, sems = refs[-3:]
    start = first // LANES * LANES
    share = turned.shape[2]
    copies = [
        pltpu.make_async_copy(
            sources[a].at[0, :, start : start + staged.shape[2]], staged.at[a], sems.at[a]
        )
        for a in range(4)
    ]
    for copy in copies:
        copy.start()
    for a in range(4):
        copies[a].wait()
        block = staged[a].T[first - start : last - start]
        for d in range(group):
            turned[a, d] = block[d * share : (d + 1) * share]
    me = lax.axis_index("space")
    for d in range(group):
        for a in range(4):
            outs[d][a * share : (a + 1) * share] = turned[a, me ^ d]


def temporal_pack_kernel(q, k, v, g, token, out):
    group, _, rows, _ = out.shape
    for t in range(group):
        for a, source in enumerate((q, k, v, g)):
            out[t, a] = source[0, t * rows : (t + 1) * rows]


def spatial_core_kernel(heads, *refs):
    group = (len(refs)) // 2
    messages, outs = refs[:group], refs[group:]
    whole = jnp.concatenate([m[...] for m in messages], axis=1)
    length = whole.shape[1]
    block = min(512, length)
    per = length // group
    every = range(heads)

    def mm(x, y):
        return jnp.dot(x, y, preferred_element_type=jnp.float32)

    def nt(x, y):
        return lax.dot_general(x, y, NT, preferred_element_type=jnp.float32)

    qs, ks, vs, gs = (
        [whole[(a * heads + h) * HEAD_DIM : (a * heads + h + 1) * HEAD_DIM] for h in every]
        for a in range(4)
    )
    k_rows = [x.T for x in ks]
    v_rows = [x.T for x in vs]
    dk = [jnp.zeros((HEAD_DIM, length), jnp.float32)] * heads
    dv = [jnp.zeros((HEAD_DIM, length), jnp.float32)] * heads
    dqs = [[] for h in every]
    for b in range(length // block):
        q = [x[:, b * block : (b + 1) * block] for x in qs]
        g = [x[:, b * block : (b + 1) * block] for x in gs]
        s = [mm(x, y) for x, y in zip(k_rows, q)]
        dp = [mm(x, y) for x, y in zip(v_rows, g)]
        for h in every:
            e = jnp.exp2((s[h] - jnp.max(s[h], axis=0, keepdims=True)) * EXP2_SCALE)
            p = e * (1.0 / jnp.sum(e, axis=0, keepdims=True))
            w = p.astype(jnp.bfloat16)
            delta = jnp.sum(w.astype(jnp.float32) * dp[h], axis=0, keepdims=True)
            ds = (p * (dp[h] - delta)).astype(jnp.bfloat16)
            dqs[h].append(mm(ks[h], ds))
            dk[h] += nt(q[h], ds)
            dv[h] += nt(g[h], w)
    dq = [jnp.concatenate(x, axis=1) * SCALE for x in dqs]
    dk = [x * SCALE for x in dk]
    low = jnp.concatenate(dq + dk + dv, axis=0).astype(jnp.bfloat16)
    for k in range(group):
        outs[k][...] = low[:, k * per : (k + 1) * per]


def temporal_unpack_kernel(arrived, *refs):
    outs, token, sems = refs[:3], refs[3], refs[4]
    parts, _, rows, _ = arrived.shape
    copies = [
        pltpu.make_async_copy(
            arrived.at[t, i], outs[i].at[0, t * rows : (t + 1) * rows], sems.at[t, i]
        )
        for i in range(3)
        for t in range(parts)
    ]
    for copy in copies:
        copy.start()
    token[...] = jnp.zeros_like(token)
    for copy in copies:
        copy.wait()


def spatial_unpack_kernel(first, last, group, count, *refs):
    messages, outs = refs[: group * count], refs[-5 - count : -2 - count]
    scratch, turned, sems = refs[-2 - count : -2], refs[-2], refs[-1]
    me = lax.axis_index("space")
    places = order(OUT_ORDER, group)
    copies = []
    for i in range(3):
        blocks = []
        for c in range(count):
            rows = scratch[c].shape[2]
            for k, d in enumerate(places):
                scratch[c][i, me ^ d] = messages[c * group + k][i * rows : (i + 1) * rows]
            blocks.append(scratch[c][i].reshape(group * rows, scratch[c].shape[3]))
        turned[i] = jnp.concatenate(blocks, axis=0)[first:last].T
        copies.append(
            pltpu.make_async_copy(turned.at[i], outs[i].at[0, :, first:last], sems.at[i])
        )
        copies[i].start()
    for copy in copies:
        copy.wait()


def send(arrays):
    _, tokens, width = arrays[0].shape
    group, parts = lax.axis_size("space"), lax.axis_size("tm")
    heads_here = width // HEAD_DIM // group
    split = SPLIT if sum(SPLIT) == heads_here else (heads_here,)
    chunks = len(split)
    rows = tokens // parts
    hbm, vmem = pl.BlockSpec(memory_space=pltpu.HBM), pl.BlockSpec(memory_space=pltpu.VMEM)
    later = pl.BlockSpec(memory_space=pl.ANY)

    def pack(c, *after):
        share = split[c] * HEAD_DIM
        first = group * HEAD_DIM * sum(split[:c])
        last = first + group * share
        span = -(-last // LANES) * LANES - first // LANES * LANES
        return call(
            f"pack_spatial{c}",
            functools.partial(spatial_pack_kernel, first, last, group),
            [bf16(4 * share, tokens)] * group,
            in_specs=[hbm] * 4 + [later] * len(after),
            scratch=[
                pltpu.VMEM((4, tokens, span), jnp.bfloat16),
                pltpu.VMEM((4, group, share, tokens), jnp.bfloat16),
                pltpu.SemaphoreType.DMA((4,)),
            ],
        )(*arrays[:4], *after)

    messages = pack(0)
    if rows % 16 == 0:
        slices = call(
            "pack_temporal",
            temporal_pack_kernel,
            bf16(parts, 4, rows, width),
            in_specs=[vmem] * 4 + [later],
        )(*arrays[4:], messages[0])
    else:
        slices = jnp.stack([x.reshape(parts, rows, width) for x in arrays[4:]], axis=1)
    for c in range(1, chunks):
        messages += pack(c, slices)
    spatial = []
    for c in range(chunks):
        mine = messages[c * group : (c + 1) * group]
        spatial.append([mine[0]] + [swap(mine[d], "space", d) for d in range(1, group)])
    return spatial, lax.all_to_all(slices, "tm", 0, 0, tiled=True)


def order(far, group):
    return [0, *(far if len(far) == group - 1 else range(1, group))]


def spatial_core(arrived, first):
    if not arrived:
        return []
    group = len(arrived[0])
    places = order(IN_ORDER, group)
    rows, tokens = arrived[0][0].shape
    heads = rows // (4 * HEAD_DIM)
    length = group * tokens
    results = []
    for c, messages in enumerate(arrived):
        results.append(
            call(
            f"core_spatial{first + c}",
            functools.partial(spatial_core_kernel, heads),
            [bf16(3 * heads * HEAD_DIM, tokens)] * group,
            cost=1.2 * heads * (length / 512) ** 2,
        )(*[messages[d] for d in places])
        )
    return [[chunk[places.index(d)] for d in range(group)] for chunk in results]


def give_back(spatial, temporal, width):
    chunks, group = len(spatial), len(spatial[0])
    tokens = spatial[0][0].shape[1]
    parts, _, rows, _ = temporal.shape
    places = order(OUT_ORDER, group)
    messages = [
        [mine[d] if d == 0 else swap(mine[d], "space", d) for d in places] for mine in spatial
    ]
    arrived = lax.all_to_all(temporal, "tm", 0, 0, tiled=True)
    hbm, vmem = pl.BlockSpec(memory_space=pltpu.HBM), pl.BlockSpec(memory_space=pltpu.VMEM)
    later = pl.BlockSpec(memory_space=pl.ANY)
    whole = [bf16(1, tokens, width)] * 3

    def unpack(name, first, last, mine, into, *after):
        n = len(mine) * group
        return call(
            name,
            functools.partial(spatial_unpack_kernel, first, last, group, len(mine)),
            whole,
            in_specs=[vmem] * n + [hbm] * len(into) + [later] * len(after),
            out_specs=[hbm] * 3,
            input_output_aliases={n + i: i for i in range(len(into))},
            scratch=[
                pltpu.VMEM((3, group, row[0].shape[0] // 3, tokens), jnp.bfloat16) for row in mine
            ]
            + [
                pltpu.VMEM((3, tokens, last - first), jnp.bfloat16),
                pltpu.SemaphoreType.DMA((3,)),
            ],
        )(*[m for row in mine for m in row], *into, *after)

    edge, begun = 0, []
    if chunks > 1:
        edge = (width - group * spatial[-1][0].shape[0] // 3) // LANES * LANES
        begun = unpack("unpack_early", 0, edge, messages[:-1], [])
    if rows % 16 == 0:
        *others, token = call(
            "unpack_temporal",
            temporal_unpack_kernel,
            whole + [bf16(16, LANES)],
            in_specs=[later],
            out_specs=[hbm] * 3 + [vmem],
            scratch=[pltpu.SemaphoreType.DMA((parts, 3))],
        )(arrived)
        after = [token]
    else:
        others = [arrived[:, i].reshape(1, tokens, width) for i in range(3)]
        after = []
    done = unpack("unpack", edge, width, messages, begun, *after)
    return list(done) + list(others)


def temporal_core_kernel(messages, *refs):
    out = refs[-1]
    group, _, tok, width = messages.shape
    total = group * tok
    arrays = [
        jnp.concatenate([messages[t, a] for t in range(group)], axis=0) for a in range(4)
    ]
    row = lax.broadcasted_iota(jnp.int32, (total, total), 0)
    col = lax.broadcasted_iota(jnp.int32, (total, total), 1)
    same = lax.rem(row, tok) == lax.rem(col, tok)
    lane = lax.broadcasted_iota(jnp.int32, (total, LANES), 1)
    tiles = width // LANES
    sums = [[[] for _ in range(tiles)] for _ in range(3)]

    def flush(t):
        for i in range(3):
            left = [x for x, _ in sums[i][t]]
            right = jnp.concatenate([y for _, y in sums[i][t]], axis=0)
            if i == 0:
                lhs = jnp.concatenate(left, axis=0)
                value = lax.dot_general(lhs, right, TN, preferred_element_type=jnp.float32)
            else:
                lhs = jnp.concatenate(left, axis=1)
                value = jnp.dot(lhs, right, preferred_element_type=jnp.float32)
            if i < 2:
                value = value * SCALE
            low = value.astype(jnp.bfloat16)
            for k in range(group):
                out[k, i, :, t * LANES : (t + 1) * LANES] = low[k * tok : (k + 1) * tok]

    def part(a, h, t, masked=True):
        block = arrays[a][:, t * LANES : (t + 1) * LANES]
        if not masked:
            return block
        low = h * HEAD_DIM - t * LANES
        keep = (lane >= low) & (lane < low + HEAD_DIM)
        return jnp.where(keep, block, jnp.zeros_like(block))

    def wide(parts):
        return jnp.concatenate(parts, axis=1)

    heads = width // HEAD_DIM
    for start in range(0, heads, HEAD_GROUP):
        batch = range(start, min(start + HEAD_GROUP, heads))
        spans = [range(h * HEAD_DIM // LANES, ((h + 1) * HEAD_DIM - 1) // LANES + 1) for h in batch]
        qm = [[part(0, h, t) for t in span] for h, span in zip(batch, spans)]
        km = [[part(1, h, t) for t in span] for h, span in zip(batch, spans)]
        gm = [[part(3, h, t) for t in span] for h, span in zip(batch, spans)]
        vs = [[part(2, h, t, False) for t in span] for h, span in zip(batch, spans)]
        s = [
            lax.dot_general(wide(x), wide(y), NT, preferred_element_type=jnp.float32)
            for x, y in zip(km, qm)
        ]
        dp = [
            lax.dot_general(wide(x), wide(y), NT, preferred_element_type=jnp.float32)
            for x, y in zip(vs, gm)
        ]
        s = [jnp.where(same, x, -1e30) for x in s]
        e = [jnp.exp2((x - jnp.max(x, axis=0, keepdims=True)) * EXP2_SCALE) for x in s]
        p = [x * (1.0 / jnp.sum(x, axis=0, keepdims=True)) for x in e]
        w = [x.astype(jnp.bfloat16) for x in p]
        delta = [
            jnp.sum(x.astype(jnp.float32) * y, axis=0, keepdims=True) for x, y in zip(w, dp)
        ]
        ds = [(x * (y - z)).astype(jnp.bfloat16) for x, y, z in zip(p, dp, delta)]
        for n, h in enumerate(batch):
            for j, t in enumerate(spans[n]):
                sums[0][t].append((ds[n], km[n][j]))
                sums[1][t].append((ds[n], qm[n][j]))
                sums[2][t].append((w[n], gm[n][j]))
                if (t + 1) * LANES <= (h + 1) * HEAD_DIM:
                    flush(t)


def temporal_core(arrived, after):
    group, _, rows, width = arrived.shape
    return call(
        "core_temporal",
        temporal_core_kernel,
        bf16(group, 3, rows, width),
        cost=3.4,
        in_specs=[pl.BlockSpec(memory_space=pltpu.VMEM)]
        + [pl.BlockSpec(memory_space=pl.ANY)] * len(after),
    )(arrived, *after)


def shards(*arrays):
    width = arrays[0].shape[2]
    spatial, temporal = send(arrays)
    cut = min(AHEAD, len(spatial))
    done = spatial_core(spatial[:cut], 0)
    after = [done[-1][0]]
    if cut < len(spatial):
        after += [spatial[cut][d] for d in GATE]
    results = temporal_core(temporal, after)
    if cut < len(spatial):
        spatial[cut][0], _ = lax.optimization_barrier((spatial[cut][0], results))
        done += spatial_core(spatial[cut:], cut)
    return tuple(give_back(done, results, width))


def solution(mesh):
    placed = P("tm", "space", None)
    return jax.shard_map(
        shards,
        mesh=mesh,
        in_specs=(placed,) * 8,
        out_specs=(placed,) * 6,
        check_vma=False,
    )
```
